256 devices in a mesh: row: 16 (over y, x), col: 16 (over z, core).
Axes of the slice: x: 4, y: 4, z: 8, core: 2. Of those that a mesh axis runs over, the one named last changes fastest.
Arguments:
- kernel_matrix: float32 [16384, 16384], P('row', 'col'), may hold values from -0.04 to 32, as said below
Outputs:
- factored: float32 [16384, 16384], P('row', 'col')
The draws below stay inside these ranges and needn't reach their ends.
Inputs may be any that keep to these rules, and one draw needn't show every extreme that they name: kernel_matrix's logical matrix is symmetric positive definite with eigenvalues of 0.1 or more.
All inputs are finite; a program needn't handle non-finite values.
Results may differ from the reference program's by a relative error of at most 0.00017.
Values sent between devices are 32-bit elements; how exact they have to be, the bound alone decides.
No kernel may reach another device: no remote copies, remote signals or barrier semaphores. Data moves between devices by JAX's collectives and lax.ppermute only.
A program may use at most 64 MiB of HBM per device.

```python
import jax
import jax.numpy as jnp
from jax import lax

ORDER = 16384
BLOCK = 128
PANELS = 4
N_ROW = 16
N_COL = 16


def draw_kernel_matrix(key, part):
    key = jax.random.fold_in(key, 11)
    key_points, key_noise, key_rough = jax.random.split(key, 3)
    points = jax.random.uniform(key_points, (ORDER, 3), dtype=jnp.float32)
    variances = 2.0 * jnp.exp(jax.random.uniform(key_noise, (ORDER,), dtype=jnp.float32) * jnp.log(3.0))
    distance = (points[:, None, 0] - points[None, :, 0]) ** 2
    distance = distance + (points[:, None, 1] - points[None, :, 1]) ** 2
    distance = distance + (points[:, None, 2] - points[None, :, 2]) ** 2
    rough = jax.random.uniform(key_rough, (ORDER, ORDER), dtype=jnp.float32, minval=-0.01, maxval=0.01)
    kernel = jnp.exp(distance * -8.0) + 0.5 * (rough + rough.T)
    indices = jnp.arange(ORDER)
    kernel = kernel.at[indices, indices].add(variances)
    row_blocks = ORDER // (BLOCK * N_ROW)
    col_blocks = ORDER // (BLOCK * N_COL)
    stored = kernel.reshape(row_blocks, N_ROW, BLOCK, ORDER).transpose(1, 0, 2, 3).reshape(ORDER, ORDER)
    stored = stored.reshape(ORDER, col_blocks, N_COL, BLOCK).transpose(0, 2, 1, 3).reshape(ORDER, ORDER)
    return stored.astype(jnp.float32)


def setup_inputs(seed: int = 0) -> dict:
    seeds = jax.random.split(jax.random.key(seed), 2)
    kernel_matrix = draw_kernel_matrix(jax.random.fold_in(seeds[1], 71), 0)
    return {"kernel_matrix": kernel_matrix}


def unstore(stored, row_count, col_count):
    row_blocks = ORDER // (BLOCK * row_count)
    col_blocks = ORDER // (BLOCK * col_count)
    logical = stored.reshape(row_count, row_blocks, BLOCK, ORDER).transpose(1, 0, 2, 3).reshape(ORDER, ORDER)
    return logical.reshape(ORDER, col_count, col_blocks, BLOCK).transpose(0, 2, 1, 3).reshape(ORDER, ORDER)

def restore(logical, row_count, col_count):
    row_blocks = ORDER // (BLOCK * row_count)
    col_blocks = ORDER // (BLOCK * col_count)
    stored = logical.reshape(row_blocks, row_count, BLOCK, ORDER).transpose(1, 0, 2, 3).reshape(ORDER, ORDER)
    return stored.reshape(ORDER, col_blocks, col_count, BLOCK).transpose(0, 2, 1, 3).reshape(ORDER, ORDER)

def reference(kernel_matrix):
    matrix = unstore(kernel_matrix, N_ROW, N_COL)
    identity = jnp.eye(BLOCK, dtype=jnp.float32)
    block_ids = (jnp.arange(ORDER, dtype=jnp.int32) // BLOCK)[:, None]
    panels = []
    for panel_id in range(PANELS):
        offset = panel_id * BLOCK
        column = matrix[:, offset:offset + BLOCK]
        factor = jnp.linalg.cholesky(matrix[offset:offset + BLOCK, offset:offset + BLOCK])
        inverse = jax.scipy.linalg.solve_triangular(factor, identity, lower=True)
        product = lax.dot_general(column.astype(jnp.float32), inverse.astype(jnp.float32), (((1,), (1,)), ((), ())), precision=lax.Precision.HIGHEST, preferred_element_type=jnp.float32)
        tiled = jnp.tile(factor, (ORDER // BLOCK, 1))
        panel = jnp.where(block_ids < panel_id, jnp.zeros_like(product), jnp.where(block_ids == panel_id, tiled, product))
        matrix = matrix - lax.dot_general(panel.astype(jnp.float32), panel.astype(jnp.float32), (((1,), (1,)), ((), ())), precision=lax.Precision.HIGHEST, preferred_element_type=jnp.float32)
        panels.append(panel)
    span = PANELS * BLOCK
    matrix = matrix.at[:, :span].set(jnp.concatenate(panels, axis=1))
    matrix = matrix.at[:span, span:].set(jnp.zeros((span, ORDER - span), dtype=jnp.float32))
    return restore(matrix, N_ROW, N_COL)
```

```python
import jax
import jax.numpy as jnp
from jax import lax
from jax.experimental import pallas as pl
from jax.experimental.pallas import tpu as pltpu
from jax.sharding import Mesh, PartitionSpec as P

BLOCK = 128
PANELS = 4
SPAN = BLOCK * PANELS
SUB = 8
F32 = jnp.float32
BF16 = jnp.bfloat16


def exact_dot(left, right, left_dim, right_dim):
    return lax.dot_general(
        left,
        right,
        (((left_dim,), (right_dim,)), ((), ())),
        precision=lax.Precision.HIGHEST,
        preferred_element_type=F32,
    )


def split(value):
    high = value.astype(BF16)
    low = (value - high.astype(F32)).astype(BF16)
    return high, low


def split_dot(left, right, left_dim, right_dim):
    def dot(a, b):
        return lax.dot_general(
            a, b, (((left_dim,), (right_dim,)), ((), ())), preferred_element_type=F32
        )

    return dot(left[0], right[0]) + (dot(left[0], right[1]) + dot(left[1], right[0]))


def lane_fill(value, lane):
    return jnp.broadcast_to(value[:, lane : lane + 1], (SUB, BLOCK))


def row_fill(value, row):
    return jnp.broadcast_to(value[row : row + 1, :], (SUB, BLOCK))


def eliminate(a, e):
    a, e = list(a), list(e)
    groups = len(a)
    sub = lax.broadcasted_iota(jnp.int32, (SUB, BLOCK), 0)
    for c in range(groups):
        base = SUB * c
        cols = {g: [lane_fill(a[g], base + j) for j in range(SUB)] for g in range(c, groups)}
        s = [[row_fill(cols[c][j], i) if i >= j else None for j in range(SUB)] for i in range(SUB)]
        ra = [row_fill(a[c], j) for j in range(SUB)]
        re = [row_fill(e[c], j) for j in range(SUB)]
        for j in range(SUB):
            inv = lax.rsqrt(s[j][j])
            for i in range(j + 1, SUB):
                s[i][j] = s[i][j] * inv
            for k in range(j + 1, SUB):
                for i in range(k, SUB):
                    s[i][k] = s[i][k] - s[i][j] * s[k][j]
            ra[j] = ra[j] * inv
            re[j] = re[j] * inv
            for k in range(j + 1, SUB):
                ra[k] = ra[k] - s[k][j] * ra[j]
                re[k] = re[k] - s[k][j] * re[j]
            for g in range(c + 1, groups):
                cols[g][j] = cols[g][j] * inv
                for k in range(j + 1, SUB):
                    cols[g][k] = cols[g][k] - cols[g][j] * s[k][j]
                a[g] = a[g] - cols[g][j] * ra[j]
                e[g] = e[g] - cols[g][j] * re[j]
        ua, ue = ra[0], re[0]
        for j in range(1, SUB):
            ua = jnp.where(sub == j, ra[j], ua)
            ue = jnp.where(sub == j, re[j], ue)
        a[c], e[c] = ua, ue
    return a, e


def head_kernel(place, r0, r1, r2, r3, o0, o1, o2, o3, u_ref, v_ref):
    x, c = place[1], place[3]
    for step, (own, other) in enumerate(((r0, o0), (r1, o1), (r2, o2), (r3, o3))):
        rows = pl.ds(pl.multiple_of(((x - step + PANELS) % PANELS) * BLOCK, BLOCK), BLOCK)
        for half in range(2):
            lanes = slice(half * BLOCK, (half + 1) * BLOCK)
            mine = pl.ds(pl.multiple_of((c + 2 * half) * BLOCK, BLOCK), BLOCK)
            theirs = pl.ds(pl.multiple_of((1 - c + 2 * half) * BLOCK, BLOCK), BLOCK)
            u_ref[rows, mine] = own[:, lanes]
            u_ref[rows, theirs] = other[:, lanes]
    row = lax.broadcasted_iota(jnp.int32, (BLOCK, BLOCK), 0)
    col = lax.broadcasted_iota(jnp.int32, (BLOCK, BLOCK), 1)
    eye = (row == col).astype(F32)
    all_rows = lax.broadcasted_iota(jnp.int32, (SPAN, SPAN), 0)
    all_cols = lax.broadcasted_iota(jnp.int32, (SPAN, SPAN), 1)
    v_ref[...] = (all_rows == all_cols).astype(F32)
    lane = lax.broadcasted_iota(jnp.int32, (BLOCK, SPAN), 1)

    def panel(k, carry):
        at = pl.multiple_of(k * BLOCK, BLOCK)
        here = pl.ds(at, BLOCK)
        block = u_ref[here, here]
        groups = range(0, BLOCK, SUB)
        a, e = eliminate([block[g : g + SUB] for g in groups], [eye[g : g + SUB] for g in groups])
        factor = jnp.where(row <= col, jnp.concatenate(a, 0), 0.0)
        inverse = jnp.where(row >= col, jnp.concatenate(e, 0), 0.0)
        upper = exact_dot(inverse, u_ref[here, :], 1, 0)
        lower = exact_dot(inverse, v_ref[here, :], 1, 0)
        u_ref[here, :] = upper
        v_ref[here, :] = lower
        u_ref[here, here] = factor
        later = jnp.where(lane >= at + BLOCK, upper, 0.0)
        u_ref[...] -= exact_dot(later, upper, 0, 0)
        v_ref[...] -= exact_dot(later, lower, 0, 0)
        return carry

    lax.fori_loop(0, PANELS, panel, 0)
    u_ref[...] = jnp.where(all_rows <= all_cols, u_ref[...], 0.0)


def factor_head(place, own, other):
    shape = jax.ShapeDtypeStruct((SPAN, SPAN), F32)
    vmem = pl.BlockSpec(memory_space=pltpu.VMEM)
    return pl.pallas_call(
        head_kernel,
        out_shape=[shape, shape],
        in_specs=[pl.BlockSpec(memory_space=pltpu.SMEM)] + [vmem] * 8,
        out_specs=[vmem, vmem],
        compiler_params=pltpu.CompilerParams(vmem_limit_bytes=48 * 2**20),
    )(place, *own, *other)


TILE = 256


def update_kernel(place, a_ref, own, other, cols, u_ref, v_ref, out_ref, w_hi, w_lo, v_hi, v_lo):
    y, x, z, c = place[0], place[1], place[2], place[3]
    t = pl.program_id(0)

    @pl.when(t == 0)
    def _():
        values = cols[...]
        column = jnp.concatenate(
            [values[:, k].reshape(BLOCK, values.shape[-1]) for k in range(PANELS)], 0
        )
        high, low = split(split_dot(split(v_ref[...]), split(column), 1, 0))
        w_hi[...] = high
        w_lo[...] = low
        for slot, k in enumerate((c, c + 2, 1 - c, 3 - c)):
            piece = v_ref[:, pl.ds(pl.multiple_of(k * BLOCK, BLOCK), BLOCK)]
            high, low = split(piece)
            v_hi[:, slot * BLOCK : (slot + 1) * BLOCK] = high
            v_lo[:, slot * BLOCK : (slot + 1) * BLOCK] = low

    first = (z + t) % 8
    second = (z - 1 - t + 8) % 8
    rows = jnp.concatenate([own[first], own[second], other[first], other[second]], 1)
    panel = split_dot(split(rows), (v_hi[...], v_lo[...]), 1, 1)
    out_ref[...] = a_ref[...] - split_dot(split(panel), (w_hi[...], w_lo[...]), 1, 0)
    q = 2 * z + c
    for k in range(PANELS):

        @pl.when(q == k)
        def _():
            out_ref[:, :BLOCK] = panel[:, k * BLOCK : (k + 1) * BLOCK]

    @pl.when((t == 0) & (y == 0))
    def _():
        out_ref[:BLOCK, :] = jnp.zeros((BLOCK, out_ref.shape[1]), F32)

    @pl.when((t == 0) & (y == 0) & (q < PANELS))
    def _():
        at_row = pl.ds(pl.multiple_of(jnp.minimum(q, PANELS - 1) * BLOCK, BLOCK), BLOCK)
        at_col = pl.ds(pl.multiple_of(x * BLOCK, BLOCK), BLOCK)
        out_ref[:BLOCK, :BLOCK] = u_ref[at_row, at_col].T


def update(place, matrix, own, other, cols, upper, inverse):
    rows, width = matrix.shape
    vmem = pl.BlockSpec(memory_space=pltpu.VMEM)
    tile = pl.BlockSpec((TILE, width), lambda t: (t, 0))
    return pl.pallas_call(
        update_kernel,
        grid=(rows // TILE,),
        out_shape=jax.ShapeDtypeStruct(matrix.shape, F32),
        in_specs=[pl.BlockSpec(memory_space=pltpu.SMEM), tile] + [vmem] * 5,
        out_specs=tile,
        scratch_shapes=[
            pltpu.VMEM((SPAN, width), BF16),
            pltpu.VMEM((SPAN, width), BF16),
            pltpu.VMEM((SPAN, SPAN), BF16),
            pltpu.VMEM((SPAN, SPAN), BF16),
        ],
        compiler_params=pltpu.CompilerParams(vmem_limit_bytes=56 * 2**20),
    )(place, matrix, own, other, cols, upper, inverse)


def send(value, axis, pairs):
    return lax.ppermute(value, axis, pairs)


def shift(value, axis, step):
    size = lax.axis_size(axis)
    return lax.ppermute(value, axis, [(i, (i + step) % size) for i in range(size)])


def swap(value):
    return lax.ppermute(value, "core", [(0, 1), (1, 0)])


def shards(matrix):
    y, x = lax.axis_index("y"), lax.axis_index("x")
    z, c = lax.axis_index("z"), lax.axis_index("core")
    place = jnp.stack([y, x, z, c]).astype(jnp.int32)
    depth = lax.axis_size("z")

    head = matrix[:BLOCK, :BLOCK]
    got = {m: send(head, "z", [(0, m), (1, (m + 1) % depth)]) for m in range(1, depth)}
    first, second = head, head
    for m in range(1, depth):
        first = jnp.where(z == m, got[m], first)
        second = jnp.where(z == (m + 1) % depth, got[m], second)
    pair = jnp.concatenate([first, second], 1)
    for m, value in enumerate([send(pair, "y", [(0, m)]) for m in (1, 2, 3)], 1):
        pair = jnp.where(y == m, value, pair)
    own = [pair] + [shift(pair, "x", s) for s in (1, 2, 3)]
    other = [swap(value) for value in own]
    upper, inverse = factor_head(place, own, other)

    lead = matrix[:, :BLOCK]
    quarter = lead.shape[0] // 4
    mine = lead[:quarter]
    for m in (1, 2, 3):
        value = send(lead[m * quarter : (m + 1) * quarter], "z", [(0, depth - m), (1, 1 + m)])
        mine = jnp.where((z == depth - m) | (z == 1 + m), value, mine)
    rows = jnp.stack([mine] + [shift(mine, "z", s) for s in range(1, depth)])
    rows_other = swap(rows)

    top = matrix[:BLOCK]
    slab = BLOCK // 4
    part = top[:slab]
    for m in (1, 2, 3):
        value = send(top[m * slab : (m + 1) * slab], "y", [(0, m)])
        part = jnp.where(y == m, value, part)
    cols = lax.all_gather(part, ("y", "x")).reshape(4, 4, slab, top.shape[1])
    cols = cols.reshape(4, 4, slab, top.shape[1])
    return update(place, matrix, rows, rows_other, cols, upper, inverse)


def solution(mesh):
    grid = Mesh(mesh.devices.reshape(4, 4, 8, 2), ("y", "x", "z", "core"))
    spec = P(("y", "x"), ("z", "core"))
    return jax.shard_map(shards, mesh=grid, in_specs=(spec,), out_specs=spec, check_vma=False)
```

```python
import jax
import jax.numpy as jnp
from jax import lax
from jax.experimental import pallas as pl
from jax.experimental.pallas import tpu as pltpu
from jax.sharding import Mesh, PartitionSpec as P

BLOCK = 128
PANELS = 4
SPAN = BLOCK * PANELS
SUB = 8
F32 = jnp.float32
BF16 = jnp.bfloat16


def exact_dot(left, right, left_dim, right_dim):
    return lax.dot_general(
        left,
        right,
        (((left_dim,), (right_dim,)), ((), ())),
        precision=lax.Precision.HIGHEST,
        preferred_element_type=F32,
    )


def split(value):
    high = value.astype(BF16)
    low = (value - high.astype(F32)).astype(BF16)
    return high, low


def split_dot(left, right, left_dim, right_dim):
    def dot(a, b):
        return lax.dot_general(
            a, b, (((left_dim,), (right_dim,)), ((), ())), preferred_element_type=F32
        )

    return dot(left[0], right[0]) + (dot(left[0], right[1]) + dot(left[1], right[0]))


def lane_fill(value, lane):
    return jnp.broadcast_to(value[:, lane : lane + 1], (SUB, BLOCK))


def row_fill(value, row):
    return jnp.broadcast_to(value[row : row + 1, :], (SUB, BLOCK))


def eliminate(a, e):
    a, e = list(a), list(e)
    groups = len(a)
    sub = lax.broadcasted_iota(jnp.int32, (SUB, BLOCK), 0)
    for c in range(groups):
        base = SUB * c
        cols = {g: [lane_fill(a[g], base + j) for j in range(SUB)] for g in range(c, groups)}
        s = [[row_fill(cols[c][j], i) if i >= j else None for j in range(SUB)] for i in range(SUB)]
        ra = [row_fill(a[c], j) for j in range(SUB)]
        re = [row_fill(e[c], j) for j in range(SUB)]
        for j in range(SUB):
            inv = lax.rsqrt(s[j][j])
            for i in range(j + 1, SUB):
                s[i][j] = s[i][j] * inv
            for k in range(j + 1, SUB):
                for i in range(k, SUB):
                    s[i][k] = s[i][k] - s[i][j] * s[k][j]
            ra[j] = ra[j] * inv
            re[j] = re[j] * inv
            for k in range(j + 1, SUB):
                ra[k] = ra[k] - s[k][j] * ra[j]
                re[k] = re[k] - s[k][j] * re[j]
            for g in range(c + 1, groups):
                cols[g][j] = cols[g][j] * inv
                for k in range(j + 1, SUB):
                    cols[g][k] = cols[g][k] - cols[g][j] * s[k][j]
                a[g] = a[g] - cols[g][j] * ra[j]
                e[g] = e[g] - cols[g][j] * re[j]
        ua, ue = ra[0], re[0]
        for j in range(1, SUB):
            ua = jnp.where(sub == j, ra[j], ua)
            ue = jnp.where(sub == j, re[j], ue)
        a[c], e[c] = ua, ue
    return a, e


def head_kernel(place, own, other, u_ref, v_ref):
    x, c = place[1], place[3]
    half = SPAN // 2
    for step in range(PANELS):
        rows = pl.ds(pl.multiple_of(((x - step + PANELS) % PANELS) * BLOCK, BLOCK), BLOCK)
        u_ref[rows, pl.ds(pl.multiple_of(c * half, half), half)] = own[step]
        u_ref[rows, pl.ds(pl.multiple_of((1 - c) * half, half), half)] = other[step]
    row = lax.broadcasted_iota(jnp.int32, (BLOCK, BLOCK), 0)
    col = lax.broadcasted_iota(jnp.int32, (BLOCK, BLOCK), 1)
    eye = (row == col).astype(F32)
    all_rows = lax.broadcasted_iota(jnp.int32, (SPAN, SPAN), 0)
    all_cols = lax.broadcasted_iota(jnp.int32, (SPAN, SPAN), 1)
    v_ref[...] = (all_rows == all_cols).astype(F32)
    lane = lax.broadcasted_iota(jnp.int32, (BLOCK, SPAN), 1)

    def panel(k, carry):
        at = pl.multiple_of(k * BLOCK, BLOCK)
        here = pl.ds(at, BLOCK)
        block = u_ref[here, here]
        groups = range(0, BLOCK, SUB)
        a, e = eliminate([block[g : g + SUB] for g in groups], [eye[g : g + SUB] for g in groups])
        factor = jnp.where(row <= col, jnp.concatenate(a, 0), 0.0)
        inverse = jnp.where(row >= col, jnp.concatenate(e, 0), 0.0)
        upper = exact_dot(inverse, u_ref[here, :], 1, 0)
        lower = exact_dot(inverse, v_ref[here, :], 1, 0)
        u_ref[here, :] = upper
        v_ref[here, :] = lower
        u_ref[here, here] = factor
        later = jnp.where(lane >= at + BLOCK, upper, 0.0)
        u_ref[...] -= exact_dot(later, upper, 0, 0)
        v_ref[...] -= exact_dot(later, lower, 0, 0)
        return carry

    lax.fori_loop(0, PANELS, panel, 0)
    u_ref[...] = jnp.where(all_rows <= all_cols, u_ref[...], 0.0)


def factor_head(place, own, other):
    shape = jax.ShapeDtypeStruct((SPAN, SPAN), F32)
    vmem = pl.BlockSpec(memory_space=pltpu.VMEM)
    return pl.pallas_call(
        head_kernel,
        out_shape=[shape, shape],
        in_specs=[pl.BlockSpec(memory_space=pltpu.SMEM), vmem, vmem],
        out_specs=[vmem, vmem],
        cost_estimate=pl.CostEstimate(
            flops=30_000_000_000, transcendentals=0, bytes_accessed=4 * 2**20
        ),
        compiler_params=pltpu.CompilerParams(vmem_limit_bytes=48 * 2**20),
    )(place, own, other)


TILE = 256


def update_kernel(
    place, a_ref, own, other, left0, left1, left2, left3, right0, right1, right2, right3, u_ref, v_ref,
    out_ref, column, w_hi, w_lo, v_hi, v_lo,
):
    y, x, z, c = place[0], place[1], place[2], place[3]
    t = pl.program_id(0)

    @pl.when(t == 0)
    def _():
        slab, half = left0.shape[1:]
        for i, (left, right) in enumerate(
            ((left0, right0), (left1, right1), (left2, right2), (left3, right3))
        ):
            for j in range(4):
                at = ((x - j + 4) % 4) * BLOCK + ((y - i + 4) % 4) * slab
                column[pl.ds(pl.multiple_of(at, slab), slab), :half] = left[j]
                at = ((x - i + 4) % 4) * BLOCK + ((y - j + 4) % 4) * slab
                column[pl.ds(pl.multiple_of(at, slab), slab), half:] = right[j]
        high, low = split(split_dot(split(v_ref[...]), split(column[...]), 1, 0))
        w_hi[...] = high
        w_lo[...] = low
        for slot, k in enumerate((c, c + 2, 1 - c, 3 - c)):
            piece = v_ref[:, pl.ds(pl.multiple_of(k * BLOCK, BLOCK), BLOCK)]
            high, low = split(piece)
            v_hi[:, slot * BLOCK : (slot + 1) * BLOCK] = high
            v_lo[:, slot * BLOCK : (slot + 1) * BLOCK] = low

    rows = jnp.concatenate([own[(8 - t) % 8], own[t + 1], other[(8 - t) % 8], other[t + 1]], 1)
    panel = split_dot(split(rows), (v_hi[...], v_lo[...]), 1, 1)
    out_ref[...] = a_ref[...] - split_dot(split(panel), (w_hi[...], w_lo[...]), 1, 0)
    q = 2 * z + c
    for k in range(PANELS):

        @pl.when(q == k)
        def _():
            out_ref[:, :BLOCK] = panel[:, k * BLOCK : (k + 1) * BLOCK]

    @pl.when((t == 0) & (y == 0))
    def _():
        out_ref[:BLOCK, :] = jnp.zeros((BLOCK, out_ref.shape[1]), F32)

    @pl.when((t == 0) & (y == 0) & (q < PANELS))
    def _():
        at_row = pl.ds(pl.multiple_of(jnp.minimum(q, PANELS - 1) * BLOCK, BLOCK), BLOCK)
        at_col = pl.ds(pl.multiple_of(x * BLOCK, BLOCK), BLOCK)
        out_ref[:BLOCK, :BLOCK] = u_ref[at_row, at_col].T


def update(place, matrix, own, other, lefts, rights, upper, inverse):
    rows, width = matrix.shape
    vmem = pl.BlockSpec(memory_space=pltpu.VMEM)
    tile = pl.BlockSpec((TILE, width), lambda t: (t, 0))
    return pl.pallas_call(
        update_kernel,
        grid=(rows // TILE,),
        out_shape=jax.ShapeDtypeStruct(matrix.shape, F32),
        in_specs=[pl.BlockSpec(memory_space=pltpu.SMEM), tile] + [vmem] * 12,
        out_specs=tile,
        scratch_shapes=[
            pltpu.VMEM((SPAN, width), F32),
            pltpu.VMEM((SPAN, width), BF16),
            pltpu.VMEM((SPAN, width), BF16),
            pltpu.VMEM((SPAN, SPAN), BF16),
            pltpu.VMEM((SPAN, SPAN), BF16),
        ],
        compiler_params=pltpu.CompilerParams(vmem_limit_bytes=56 * 2**20),
    )(place, matrix, own, other, *lefts, *rights, upper, inverse)


def send(value, axis, pairs):
    return lax.ppermute(value, axis, pairs)


def shift(value, axis, step):
    size = lax.axis_size(axis)
    return lax.ppermute(value, axis, [(i, (i + step) % size) for i in range(size)])


def swap(value):
    return lax.ppermute(value, "core", [(0, 1), (1, 0)])


def shards(matrix):
    y, x = lax.axis_index("y"), lax.axis_index("x")
    z, c = lax.axis_index("z"), lax.axis_index("core")
    place = jnp.stack([y, x, z, c]).astype(jnp.int32)
    depth = lax.axis_size("z")

    head = matrix[:BLOCK, :BLOCK]
    twin = swap(head)
    pair = jnp.concatenate([jnp.where(c == 0, head, twin), jnp.where(c == 0, twin, head)], 1)
    pairs = [[] for _ in range(4)]
    for (source_z, source_c), targets in (
        ((0, 0), (1, 2, 3, 4)),
        ((0, 1), (7, 6, 5)),
        ((1, 0), (2, 3, 4, 5)),
        ((1, 1), (0, 7, 6)),
    ):
        for turn, target in enumerate(targets):
            pairs[turn].append((source_z * 2 + source_c, target * 2 + source_z))
    got = [lax.ppermute(pair, ("z", "core"), turn) for turn in pairs]
    mine = z == c
    pair = jnp.where(mine, pair, got[0] + got[1] + got[2] + got[3])
    got = [send(pair, "y", [(0, m)]) for m in (1, 2, 3)]
    pair = jnp.where(y == 0, pair, got[0] + got[1] + got[2])
    own = jnp.stack([pair] + [shift(pair, "x", s) for s in (1, 2, 3)])
    upper, inverse = factor_head(place, own, swap(own))

    lead = matrix[:, :BLOCK]
    quarter = lead.shape[0] // 4
    got = [
        send(lead[m * quarter : (m + 1) * quarter], "z", [(0, depth - m), (1, 1 + m)])
        for m in (1, 2, 3)
    ]
    part = jnp.where(z < 2, lead[:quarter], got[0] + got[1] + got[2])
    rows = lax.all_gather(part, "z")

    top = matrix[:BLOCK]
    slab = BLOCK // 4
    got = [send(top[m * slab : (m + 1) * slab], "y", [(0, m)]) for m in (1, 2, 3)]
    part = jnp.where(y == 0, top[:slab], got[0] + got[1] + got[2])
    half = part.shape[1] // 2
    left, right = part[:, :half], part[:, half:]
    left = jnp.stack([left] + [shift(left, "x", s) for s in (1, 2, 3)])
    right = jnp.stack([right] + [shift(right, "y", s) for s in (1, 2, 3)])
    lefts = [left] + [shift(left, "y", s) for s in (1, 2, 3)]
    rights = [right] + [shift(right, "x", s) for s in (1, 2, 3)]
    return update(place, matrix, rows, swap(rows), lefts, rights, upper, inverse)


def solution(mesh):
    grid = Mesh(mesh.devices.reshape(4, 4, 8, 2), ("y", "x", "z", "core"))
    spec = P(("y", "x"), ("z", "core"))
    return jax.shard_map(shards, mesh=grid, in_specs=(spec,), out_specs=spec, check_vma=False)
```

```python
import jax
import jax.numpy as jnp
from jax import lax
from jax.experimental import pallas as pl
from jax.experimental.pallas import tpu as pltpu
from jax.sharding import Mesh, PartitionSpec as P

BLOCK = 128
PANELS = 4
SPAN = BLOCK * PANELS
SUB = 8
F32 = jnp.float32
BF16 = jnp.bfloat16


def split(value):
    high = value.astype(BF16)
    low = (value - high.astype(F32)).astype(BF16)
    return high, low


def split_dot(left, right, left_dim, right_dim):
    def dot(a, b):
        return lax.dot_general(
            a, b, (((left_dim,), (right_dim,)), ((), ())), preferred_element_type=F32
        )

    return dot(left[0], right[0]) + (dot(left[0], right[1]) + dot(left[1], right[0]))


def lane_fill(value, lane):
    return jnp.broadcast_to(value[:, lane : lane + 1], (SUB, BLOCK))


def eliminate(a, scratch):
    a = list(a)
    groups = len(a)
    sub = lax.broadcasted_iota(jnp.int32, (SUB, BLOCK), 0)
    lane = lax.broadcasted_iota(jnp.int32, (SUB, BLOCK), 1)
    upper, lower = [None] * groups, [None] * groups
    columns = [lane_fill(a[0], j) for j in range(SUB)]

    def stored_row(at):
        return jnp.broadcast_to(scratch[at : at + 1, :], (SUB, BLOCK))

    for c in range(groups):
        base = SUB * c
        inside = (lane >= base) & (lane < base + SUB)
        at = (c % 2) * (SUB + 1 + SUB) * SUB
        scratch[at : at + SUB, :] = a[c]
        for j in range(SUB):
            scratch[at + SUB * (j + 1) : at + SUB * (j + 2), :] = columns[j]
        s = [
            [stored_row(at + SUB * (j + 1) + i) if i >= j else None for j in range(SUB)]
            for i in range(SUB)
        ]
        rows = [stored_row(at + j) for j in range(SUB)]
        units = [(lane == base + j).astype(F32) for j in range(SUB)]
        more = c + 1 < groups
        if more:
            left = [lane_fill(a[c + 1], base + j) for j in range(SUB)]
            columns = [lane_fill(a[c + 1], base + SUB + j) for j in range(SUB)]
            a[c + 1] = jnp.where(inside, 0.0, a[c + 1])
        inv, merged = [None] * SUB, [None] * SUB
        for j in range(SUB):
            inv[j] = lax.rsqrt(s[j][j])
            for i in range(j + 1, SUB):
                s[i][j] = s[i][j] * inv[j]
            for k in range(j + 1, SUB):
                for i in range(k, SUB):
                    s[i][k] = s[i][k] - s[i][j] * s[k][j]
            rows[j] = rows[j] * inv[j]
            units[j] = units[j] * inv[j]
            for k in range(j + 1, SUB):
                rows[k] = rows[k] - s[k][j] * rows[j]
                units[k] = units[k] - s[k][j] * units[j]
            merged[j] = jnp.where(inside, units[j], rows[j])
            if more:
                left[j] = left[j] * inv[j]
                for k in range(j + 1, SUB):
                    left[k] = left[k] - left[j] * s[k][j]
                a[c + 1] = a[c + 1] - left[j] * merged[j]
                spot = at + (SUB + 1 + j) * SUB
                scratch[spot : spot + SUB, :] = left[j]
                for k in range(SUB):
                    columns[k] = columns[k] - left[j] * stored_row(spot + k)
        upper[c], lower[c] = rows[0], merged[0]
        for j in range(1, SUB):
            upper[c] = jnp.where(sub == j, rows[j], upper[c])
            lower[c] = jnp.where(sub == j, merged[j], lower[c])
        if c + 2 < groups:
            solved = list(merged)
            for j in range(SUB - 1, -1, -1):
                solved[j] = solved[j] * inv[j]
                for k in range(j):
                    solved[k] = solved[k] - s[j][k] * solved[j]
            for g in range(c + 2, groups):
                value = jnp.where(inside, 0.0, a[g])
                for j in range(SUB):
                    value = value - lane_fill(a[g], base + j) * solved[j]
                a[g] = value
    return upper, lower


def split3(value):
    high = value.astype(BF16)
    rest = value - high.astype(F32)
    middle = rest.astype(BF16)
    low = (rest - middle.astype(F32)).astype(BF16)
    return high, middle, low


def stack_left(value):
    high, middle, low = split3(value)
    return jnp.concatenate([high, high, middle, middle, high, low], 1)


def stack_right(value):
    high, middle, low = split3(value)
    return jnp.concatenate([high, middle, high, middle, low, high], 0)


def stacked_dot(left, right):
    return lax.dot_general(left, right, (((1,), (0,)), ((), ())), preferred_element_type=F32)


def head_kernel(place, own, other, u_ref, v_ref, head, scratch):
    x, c = place[1], place[3]
    half = SPAN // 2
    for step in range(PANELS):
        rows = pl.ds(pl.multiple_of(((x - step + PANELS) % PANELS) * BLOCK, BLOCK), BLOCK)
        for n in range(2):
            block = slice(n * BLOCK, (n + 1) * BLOCK)
            at = pl.multiple_of(c * half + n * BLOCK, BLOCK)
            head[rows, pl.ds(at, BLOCK)] = own[step, block]
            at = pl.multiple_of((1 - c) * half + n * BLOCK, BLOCK)
            head[rows, pl.ds(at, BLOCK)] = other[step, block]
    row = lax.broadcasted_iota(jnp.int32, (BLOCK, BLOCK), 0)
    col = lax.broadcasted_iota(jnp.int32, (BLOCK, BLOCK), 1)
    spans = [slice(k * BLOCK, (k + 1) * BLOCK) for k in range(PANELS)]
    work = {(i, j): head[spans[i], spans[j]] for i in range(PANELS) for j in range(i, PANELS)}
    unit = {}
    for k in range(PANELS):
        block = work[k, k]
        upper, lower = eliminate([block[g : g + SUB] for g in range(0, BLOCK, SUB)], scratch)
        factor = jnp.where(row <= col, jnp.concatenate(upper, 0), 0.0)
        inverse = jnp.where(row >= col, jnp.concatenate(lower, 0), 0.0)
        u_ref[spans[k], spans[k]] = factor
        v_ref[spans[k], spans[k]] = inverse
        sources = [work[k, j] for j in range(k + 1, PANELS)] + [unit[k, j] for j in range(k)]
        solved = stacked_dot(stack_left(inverse), stack_right(jnp.concatenate(sources, 1)))
        pieces = [solved[:, spans[i]] for i in range(PANELS - 1)]
        right = {j: pieces[j - k - 1] for j in range(k + 1, PANELS)}
        left = {j: pieces[PANELS - 1 - k + j] for j in range(k)}
        for j, value in right.items():
            u_ref[spans[k], spans[j]] = value
        for j, value in left.items():
            v_ref[spans[k], spans[j]] = value
        left[k] = inverse
        for i in range(k + 1, PANELS):
            factors = stack_left(right[i].T)
            first = i
            if i == k + 1:
                work[i, i] = work[i, i] - stacked_dot(factors, stack_right(right[i]))
                first = i + 1
            values = [right[j] for j in range(first, PANELS)] + [left[j] for j in range(k + 1)]
            change = stacked_dot(factors, stack_right(jnp.concatenate(values, 1)))
            parts = [change[:, n * BLOCK : (n + 1) * BLOCK] for n in range(len(values))]
            for j in range(first, PANELS):
                work[i, j] = work[i, j] - parts.pop(0)
            for j in range(k + 1):
                part = parts.pop(0)
                unit[i, j] = unit[i, j] - part if (i, j) in unit else -part
    for i in range(PANELS):
        for j in range(i):
            u_ref[spans[i], spans[j]] = jnp.zeros((BLOCK, BLOCK), F32)
            v_ref[spans[j], spans[i]] = jnp.zeros((BLOCK, BLOCK), F32)


def factor_head(place, own, other):
    shape = jax.ShapeDtypeStruct((SPAN, SPAN), F32)
    vmem = pl.BlockSpec(memory_space=pltpu.VMEM)
    return pl.pallas_call(
        head_kernel,
        out_shape=[shape, shape],
        in_specs=[pl.BlockSpec(memory_space=pltpu.SMEM), vmem, vmem],
        out_specs=[vmem, vmem],
        scratch_shapes=[
            pltpu.VMEM((SPAN, SPAN), F32),
            pltpu.VMEM((2 * (2 * SUB + 1) * SUB, BLOCK), F32),
        ],
        cost_estimate=pl.CostEstimate(
            flops=30_000_000_000, transcendentals=0, bytes_accessed=4 * 2**20
        ),
        compiler_params=pltpu.CompilerParams(vmem_limit_bytes=48 * 2**20),
    )(place, own, other)


SLAB = BLOCK // 4


TILE = 256


def update_kernel(
    place, a_ref, rows0, rows1, rows2, rows3, c0, c1, c2, c3, u_ref, v_ref, out_ref, column, w_hi, w_lo, v_hi, v_lo
):
    y, x, z, c = place[0], place[1], place[2], place[3]
    t = pl.program_id(0)

    @pl.when(t == 0)
    def _():
        for late, ref in enumerate((c0, c1, c2, c3)):
            for early in range(4):
                dx = jnp.where(c == 0, early, late)
                dy = jnp.where(c == 0, late, early)
                at = ((x - dx + 4) % 4) * BLOCK + ((y - dy + 4) % 4) * SLAB
                column[pl.ds(pl.multiple_of(at, SLAB), SLAB), :] = ref[early]
        high, low = split(split_dot(split(v_ref[...]), split(column[...]), 1, 0))
        w_hi[...] = high
        w_lo[...] = low
        high, low = split(v_ref[...])
        v_hi[...] = high
        v_lo[...] = low

    rows = jnp.concatenate([rows0[0], rows1[0], rows2[0], rows3[0]], 1)
    panel = split_dot(split(rows), (v_hi[...], v_lo[...]), 1, 1)
    out_ref[...] = a_ref[...] - split_dot(split(panel), (w_hi[...], w_lo[...]), 1, 0)
    q = 2 * z + c
    for k in range(PANELS):

        @pl.when(q == k)
        def _():
            out_ref[:, :BLOCK] = panel[:, k * BLOCK : (k + 1) * BLOCK]

    @pl.when((t == 0) & (y == 0))
    def _():
        out_ref[:BLOCK, :] = jnp.zeros((BLOCK, out_ref.shape[1]), F32)

    @pl.when((t == 0) & (y == 0) & (q < PANELS))
    def _():
        at_row = pl.ds(pl.multiple_of(jnp.minimum(q, PANELS - 1) * BLOCK, BLOCK), BLOCK)
        at_col = pl.ds(pl.multiple_of(x * BLOCK, BLOCK), BLOCK)
        out_ref[:BLOCK, :BLOCK] = u_ref[at_row, at_col].T


def update(place, matrix, rows, cols, upper, inverse):
    height, width = matrix.shape
    vmem = pl.BlockSpec(memory_space=pltpu.VMEM)
    tile = pl.BlockSpec((TILE, width), lambda t: (t, 0))
    quarter = (1,) + rows.shape[1:]
    pieces = [
        pl.BlockSpec(quarter, lambda t: (2 * ((8 - t) % 8), 0, 0)),
        pl.BlockSpec(quarter, lambda t: (2 * ((8 - t) % 8) + 1, 0, 0)),
        pl.BlockSpec(quarter, lambda t: (2 * (t + 1), 0, 0)),
        pl.BlockSpec(quarter, lambda t: (2 * (t + 1) + 1, 0, 0)),
    ]
    return pl.pallas_call(
        update_kernel,
        grid=(height // TILE,),
        out_shape=jax.ShapeDtypeStruct(matrix.shape, F32),
        in_specs=[pl.BlockSpec(memory_space=pltpu.SMEM), tile] + pieces + [vmem] * 6,
        out_specs=tile,
        scratch_shapes=[
            pltpu.VMEM((SPAN, width), F32),
            pltpu.VMEM((SPAN, width), BF16),
            pltpu.VMEM((SPAN, width), BF16),
            pltpu.VMEM((SPAN, SPAN), BF16),
            pltpu.VMEM((SPAN, SPAN), BF16),
        ],
        compiler_params=pltpu.CompilerParams(vmem_limit_bytes=56 * 2**20),
    )(place, matrix, rows, rows, rows, rows, *cols, upper, inverse)


def send(value, axis, pairs):
    return lax.ppermute(value, axis, pairs)


def shift(value, axis, step):
    size = lax.axis_size(axis)
    return lax.ppermute(value, axis, [(i, (i + step) % size) for i in range(size)])


def swap(value):
    return lax.ppermute(value, "core", [(0, 1), (1, 0)])


def turn(value, step, first):
    pairs = []
    for y in range(4):
        for x in range(4):
            for core in range(2):
                to = (y, (x + step) % 4) if core == first else ((y + step) % 4, x)
                pairs.append(((y * 4 + x) * 2 + core, (to[0] * 4 + to[1]) * 2 + core))
    return lax.ppermute(value, ("y", "x", "core"), pairs)


def shards(matrix):
    y, x = lax.axis_index("y"), lax.axis_index("x")
    z, c = lax.axis_index("z"), lax.axis_index("core")
    place = jnp.stack([y, x, z, c]).astype(jnp.int32)
    depth = lax.axis_size("z")

    head = matrix[:BLOCK, :BLOCK]
    twin = swap(head)
    pair = jnp.concatenate([jnp.where(c == 0, head, twin), jnp.where(c == 0, twin, head)], 0)
    pairs = [[] for _ in range(4)]
    for (source_z, source_c), targets in (
        ((0, 0), (1, 2, 3, 4)),
        ((0, 1), (7, 6, 5)),
        ((1, 0), (2, 3, 4, 5)),
        ((1, 1), (0, 7, 6)),
    ):
        for n, target in enumerate(targets):
            pairs[n].append((source_z * 2 + source_c, target * 2 + source_z))
    got = [lax.ppermute(pair, ("z", "core"), group) for group in pairs]

    lead = matrix[:, :BLOCK]
    quarter = lead.shape[0] // 4
    sent = [
        send(lead[m * quarter : (m + 1) * quarter], "z", [(0, depth - m), (1, 1 + m)])
        for m in (1, 2, 3)
    ]
    part = jnp.where(z < 2, lead[:quarter], sent[0] + sent[1] + sent[2])
    rows = lax.all_gather(part, ("z", "core"))

    top = matrix[:BLOCK]
    sent = [send(top[m * SLAB : (m + 1) * SLAB], "y", [(0, m)]) for m in (1, 2, 3)]
    share = jnp.where(y == 0, top[:SLAB], sent[0] + sent[1] + sent[2])

    pair = jnp.where(z == c, pair, got[0] + got[1] + got[2] + got[3])
    got = [send(pair, "y", [(0, m)]) for m in (1, 2, 3)]
    some = jnp.stack([share] + [turn(share, s, 0) for s in (1, 2, 3)])
    pair = jnp.where(y == 0, pair, got[0] + got[1] + got[2])
    own = jnp.stack([pair] + [shift(pair, "x", s) for s in (1, 2, 3)])
    cols = [some] + [turn(some, s, 1) for s in (1, 2, 3)]
    upper, inverse = factor_head(place, own, swap(own))
    return update(place, matrix, rows, cols, upper, inverse)


def solution(mesh):
    grid = Mesh(mesh.devices.reshape(4, 4, 8, 2), ("y", "x", "z", "core"))
    spec = P(("y", "x"), ("z", "core"))
    return jax.shard_map(shards, mesh=grid, in_specs=(spec,), out_specs=spec, check_vma=False)
```

```python
import jax
import jax.numpy as jnp
from jax import lax
from jax.experimental import pallas as pl
from jax.experimental.pallas import tpu as pltpu
from jax.sharding import Mesh, PartitionSpec as P

BLOCK = 128
PANELS = 4
SPAN = BLOCK * PANELS
SUB = 8
F32 = jnp.float32
BF16 = jnp.bfloat16


def split(value):
    high = value.astype(BF16)
    low = (value - high.astype(F32)).astype(BF16)
    return high, low


def plain_dot(left, right, left_dim, right_dim):
    return lax.dot_general(
        left, right, (((left_dim,), (right_dim,)), ((), ())), preferred_element_type=F32
    )


def pieces_left(high, low):
    return jnp.concatenate([high, high, low], 1)


def lane_fill(value, lane):
    return jnp.broadcast_to(value[:, lane : lane + 1], (SUB, BLOCK))


def eliminate(a, scratch):
    a = list(a)
    groups = len(a)
    sub = lax.broadcasted_iota(jnp.int32, (SUB, BLOCK), 0)
    lane = lax.broadcasted_iota(jnp.int32, (SUB, BLOCK), 1)
    upper, lower = [None] * groups, [None] * groups
    columns = [lane_fill(a[0], j) for j in range(SUB)]

    def stored_row(at):
        return jnp.broadcast_to(scratch[at : at + 1, :], (SUB, BLOCK))

    for c in range(groups):
        base = SUB * c
        inside = (lane >= base) & (lane < base + SUB)
        at = (c % 2) * (SUB + 1 + SUB) * SUB
        scratch[at : at + SUB, :] = a[c]
        for j in range(SUB):
            scratch[at + SUB * (j + 1) : at + SUB * (j + 2), :] = columns[j]
        s = [
            [stored_row(at + SUB * (j + 1) + i) if i >= j else None for j in range(SUB)]
            for i in range(SUB)
        ]
        rows = [stored_row(at + j) for j in range(SUB)]
        units = [(lane == base + j).astype(F32) for j in range(SUB)]
        more = c + 1 < groups
        if more:
            left = [lane_fill(a[c + 1], base + j) for j in range(SUB)]
            columns = [lane_fill(a[c + 1], base + SUB + j) for j in range(SUB)]
            a[c + 1] = jnp.where(inside, 0.0, a[c + 1])
        inv, merged = [None] * SUB, [None] * SUB
        for j in range(SUB):
            inv[j] = lax.rsqrt(s[j][j])
            for i in range(j + 1, SUB):
                s[i][j] = s[i][j] * inv[j]
            for k in range(j + 1, SUB):
                for i in range(k, SUB):
                    s[i][k] = s[i][k] - s[i][j] * s[k][j]
            rows[j] = rows[j] * inv[j]
            units[j] = units[j] * inv[j]
            for k in range(j + 1, SUB):
                rows[k] = rows[k] - s[k][j] * rows[j]
                units[k] = units[k] - s[k][j] * units[j]
            merged[j] = jnp.where(inside, units[j], rows[j])
            if more:
                left[j] = left[j] * inv[j]
                for k in range(j + 1, SUB):
                    left[k] = left[k] - left[j] * s[k][j]
                a[c + 1] = a[c + 1] - left[j] * merged[j]
                spot = at + (SUB + 1 + j) * SUB
                scratch[spot : spot + SUB, :] = left[j]
                for k in range(SUB):
                    columns[k] = columns[k] - left[j] * stored_row(spot + k)
        upper[c], lower[c] = rows[0], merged[0]
        for j in range(1, SUB):
            upper[c] = jnp.where(sub == j, rows[j], upper[c])
            lower[c] = jnp.where(sub == j, merged[j], lower[c])
        if c + 2 < groups:
            solved = list(merged)
            for j in range(SUB - 1, -1, -1):
                solved[j] = solved[j] * inv[j]
                for k in range(j):
                    solved[k] = solved[k] - s[j][k] * solved[j]
            for g in range(c + 2, groups):
                value = jnp.where(inside, 0.0, a[g])
                for j in range(SUB):
                    value = value - lane_fill(a[g], base + j) * solved[j]
                a[g] = value
    return upper, lower


def split3(value):
    high = value.astype(BF16)
    rest = value - high.astype(F32)
    middle = rest.astype(BF16)
    low = (rest - middle.astype(F32)).astype(BF16)
    return high, middle, low


def stack_left(value):
    high, middle, low = split3(value)
    return jnp.concatenate([high, high, middle, middle, high, low], 1)


def stack_right(value):
    high, middle, low = split3(value)
    return jnp.concatenate([high, middle, high, middle, low, high], 0)


def stacked_dot(left, right):
    return lax.dot_general(left, right, (((1,), (0,)), ((), ())), preferred_element_type=F32)


def head_kernel(place, own, other, corner, v_ref, head, u_ref, scratch):
    x, c = place[1], place[3]
    half = SPAN // 2
    for step in range(PANELS):
        rows = pl.ds(pl.multiple_of(((x - step + PANELS) % PANELS) * BLOCK, BLOCK), BLOCK)
        for n in range(2):
            block = slice(n * BLOCK, (n + 1) * BLOCK)
            at = pl.multiple_of(c * half + n * BLOCK, BLOCK)
            head[rows, pl.ds(at, BLOCK)] = own[step, block]
            at = pl.multiple_of((1 - c) * half + n * BLOCK, BLOCK)
            head[rows, pl.ds(at, BLOCK)] = other[step, block]
    row = lax.broadcasted_iota(jnp.int32, (BLOCK, BLOCK), 0)
    col = lax.broadcasted_iota(jnp.int32, (BLOCK, BLOCK), 1)
    spans = [slice(k * BLOCK, (k + 1) * BLOCK) for k in range(PANELS)]
    work = {(i, j): head[spans[i], spans[j]] for i in range(PANELS) for j in range(i, PANELS)}
    unit = {}
    for k in range(PANELS):
        block = work[k, k]
        upper, lower = eliminate([block[g : g + SUB] for g in range(0, BLOCK, SUB)], scratch)
        factor = jnp.where(row <= col, jnp.concatenate(upper, 0), 0.0)
        inverse = jnp.where(row >= col, jnp.concatenate(lower, 0), 0.0)
        u_ref[spans[k], spans[k]] = factor
        v_ref[spans[k], spans[k]] = inverse
        sources = [work[k, j] for j in range(k + 1, PANELS)] + [unit[k, j] for j in range(k)]
        solved = stacked_dot(stack_left(inverse), stack_right(jnp.concatenate(sources, 1)))
        pieces = [solved[:, spans[i]] for i in range(PANELS - 1)]
        right = {j: pieces[j - k - 1] for j in range(k + 1, PANELS)}
        left = {j: pieces[PANELS - 1 - k + j] for j in range(k)}
        for j, value in right.items():
            u_ref[spans[k], spans[j]] = value
        for j, value in left.items():
            v_ref[spans[k], spans[j]] = value
        left[k] = inverse
        for i in range(k + 1, PANELS):
            factors = stack_left(right[i].T)
            first = i
            if i == k + 1:
                work[i, i] = work[i, i] - stacked_dot(factors, stack_right(right[i]))
                first = i + 1
            values = [right[j] for j in range(first, PANELS)] + [left[j] for j in range(k + 1)]
            change = stacked_dot(factors, stack_right(jnp.concatenate(values, 1)))
            parts = [change[:, n * BLOCK : (n + 1) * BLOCK] for n in range(len(values))]
            for j in range(first, PANELS):
                work[i, j] = work[i, j] - parts.pop(0)
            for j in range(k + 1):
                part = parts.pop(0)
                unit[i, j] = unit[i, j] - part if (i, j) in unit else -part
    for i in range(PANELS):
        for j in range(i):
            u_ref[spans[i], spans[j]] = jnp.zeros((BLOCK, BLOCK), F32)
            v_ref[spans[j], spans[i]] = jnp.zeros((BLOCK, BLOCK), F32)
    q = jnp.minimum(2 * place[2] + c, PANELS - 1)
    at_row = pl.ds(pl.multiple_of(q * BLOCK, BLOCK), BLOCK)
    corner[...] = u_ref[at_row, pl.ds(pl.multiple_of(x * BLOCK, BLOCK), BLOCK)].T


def factor_head(place, own, other):
    shapes = [jax.ShapeDtypeStruct((n, n), F32) for n in (BLOCK, SPAN)]
    vmem = pl.BlockSpec(memory_space=pltpu.VMEM)
    return pl.pallas_call(
        head_kernel,
        out_shape=shapes,
        in_specs=[pl.BlockSpec(memory_space=pltpu.SMEM), vmem, vmem],
        out_specs=[vmem, vmem],
        scratch_shapes=[
            pltpu.VMEM((SPAN, SPAN), F32),
            pltpu.VMEM((SPAN, SPAN), F32),
            pltpu.VMEM((2 * (2 * SUB + 1) * SUB, BLOCK), F32),
        ],
        cost_estimate=pl.CostEstimate(
            flops=30_000_000_000, transcendentals=0, bytes_accessed=4 * 2**20
        ),
        compiler_params=pltpu.CompilerParams(vmem_limit_bytes=48 * 2**20),
    )(place, own, other)


SLAB = BLOCK // 4


def after(value, ready):
    return value + ready[(slice(0, 1),) * ready.ndim].reshape((1,) * value.ndim) * 0.0


TILE = 256


def update_kernel(
    place, a_ref, rows0, rows1, rows2, rows3, c0, c1, c2, c3, corner, v_ref, out_ref, column, w_all, v_all
):
    y, x, z, c = place[0], place[1], place[2], place[3]
    t = pl.program_id(0)
    half = SPAN // 2

    @pl.when(t == 0)
    def _():
        for late, ref in enumerate((c0, c1, c2, c3)):
            for early in range(4):
                dx = jnp.where(c == 0, early, late)
                dy = jnp.where(c == 0, late, early)
                at = ((x - dx + 4) % 4) * BLOCK + ((y - dy + 4) % 4) * SLAB
                column[pl.ds(pl.multiple_of(at, SLAB), SLAB), :] = ref[early]
        v_high, v_low = split(v_ref[...])
        high, low = split(column[...])
        for i in range(2):
            rows, depth = slice(i * half, (i + 1) * half), (i + 1) * half
            left = pieces_left(v_high[rows, :depth], v_low[rows, :depth])
            right = jnp.concatenate([high[:depth], low[:depth], high[:depth]], 0)
            w_high, w_low = split(plain_dot(left, right, 1, 0))
            for n, value in enumerate((w_high, w_low, w_high)):
                w_all[n * SPAN + i * half : n * SPAN + (i + 1) * half] = value
            v_all[i, :, : 3 * depth] = jnp.concatenate(
                [v_high[rows, :depth], v_low[rows, :depth], v_high[rows, :depth]], 1
            )

    rows = jnp.concatenate([rows0[0], rows1[0], rows2[0], rows3[0]], 1)
    high, low = split(rows)
    panel = jnp.concatenate(
        [
            plain_dot(pieces_left(high[:, :half], low[:, :half]), v_all[0, :, : 3 * half], 1, 1),
            plain_dot(pieces_left(high, low), v_all[1], 1, 1),
        ],
        1,
    )
    high, low = split(panel)
    out_ref[...] = a_ref[...] - plain_dot(pieces_left(high, low), w_all[...], 1, 0)
    q = 2 * z + c
    for k in range(PANELS):

        @pl.when(q == k)
        def _():
            out_ref[:, :BLOCK] = panel[:, k * BLOCK : (k + 1) * BLOCK]

    @pl.when((t == 0) & (y == 0))
    def _():
        out_ref[:BLOCK, :] = jnp.zeros((BLOCK, out_ref.shape[1]), F32)

    @pl.when((t == 0) & (y == 0) & (q < PANELS))
    def _():
        out_ref[:BLOCK, :BLOCK] = corner[...]


def update(place, matrix, rows, cols, corner, inverse):
    height, width = matrix.shape
    vmem = pl.BlockSpec(memory_space=pltpu.VMEM)
    tile = pl.BlockSpec((TILE, width), lambda t, place: (t, 0))
    part = (1,) + rows.shape[1:]

    def whole(shape):
        return pl.BlockSpec(shape, lambda t, place: (0,) * len(shape), pipeline_mode=pl.Buffered(1))

    pieces = [
        pl.BlockSpec(part, lambda t, place: (2 * ((8 - t) % 8), 0, 0)),
        pl.BlockSpec(part, lambda t, place: (2 * ((8 - t) % 8) + 1, 0, 0)),
        pl.BlockSpec(part, lambda t, place: (2 * (t + 1), 0, 0)),
        pl.BlockSpec(part, lambda t, place: (2 * (t + 1) + 1, 0, 0)),
    ]
    return pl.pallas_call(
        update_kernel,
        out_shape=jax.ShapeDtypeStruct(matrix.shape, F32),
        grid_spec=pltpu.PrefetchScalarGridSpec(
            num_scalar_prefetch=1,
            grid=(height // TILE,),
            in_specs=[tile] + pieces + [vmem] * 4 + [vmem, vmem],
            out_specs=tile,
            scratch_shapes=[
                pltpu.VMEM((SPAN, width), F32),
                pltpu.VMEM((3 * SPAN, width), BF16),
                pltpu.VMEM((2, SPAN // 2, 3 * SPAN), BF16),
            ],
        ),
        compiler_params=pltpu.CompilerParams(vmem_limit_bytes=52 * 2**20),
    )(place, matrix, rows, rows, rows, rows, *cols, corner, inverse)


def send(value, axis, pairs):
    return lax.ppermute(value, axis, pairs)


def shift(value, axis, step):
    size = lax.axis_size(axis)
    return lax.ppermute(value, axis, [(i, (i + step) % size) for i in range(size)])


def swap(value):
    return lax.ppermute(value, "core", [(0, 1), (1, 0)])


def turn(value, step, first):
    pairs = []
    for y in range(4):
        for x in range(4):
            for core in range(2):
                to = (y, (x + step) % 4) if core == first else ((y + step) % 4, x)
                pairs.append(((y * 4 + x) * 2 + core, (to[0] * 4 + to[1]) * 2 + core))
    return lax.ppermute(value, ("y", "x", "core"), pairs)


def shards(matrix):
    y, x = lax.axis_index("y"), lax.axis_index("x")
    z, c = lax.axis_index("z"), lax.axis_index("core")
    place = jnp.stack([y, x, z, c]).astype(jnp.int32)
    depth = lax.axis_size("z")

    head = matrix[:BLOCK, :BLOCK]
    twin = swap(head)
    pair = jnp.concatenate([jnp.where(c == 0, head, twin), jnp.where(c == 0, twin, head)], 0)
    pairs = [[] for _ in range(4)]
    for (source_z, source_c), targets in (
        ((0, 0), (1, 2, 3, 4)),
        ((0, 1), (7, 6, 5)),
        ((1, 0), (2, 3, 4, 5)),
        ((1, 1), (0, 7, 6)),
    ):
        for n, target in enumerate(targets):
            pairs[n].append((source_z * 2 + source_c, target * 2 + source_z))
    got = [lax.ppermute(pair, ("z", "core"), group) for group in pairs]

    lead = matrix[:, :BLOCK]
    quarter = lead.shape[0] // 4
    sent = [
        send(lead[m * quarter : (m + 1) * quarter], "z", [(0, depth - m), (1, 1 + m)])
        for m in (1, 2, 3)
    ]
    part = jnp.where(z < 2, lead[:quarter], sent[0] + sent[1] + sent[2])
    rows = lax.all_gather(part, ("z", "core"))

    top = matrix[:BLOCK]
    sent = [send(top[m * SLAB : (m + 1) * SLAB], "y", [(0, m)]) for m in (1, 2, 3)]
    share = jnp.where(y == 0, top[:SLAB], sent[0] + sent[1] + sent[2])

    pair = jnp.where(z == c, pair, got[0] + got[1] + got[2] + got[3])
    got = [send(pair, "y", [(0, m)]) for m in (1, 2, 3)]
    some = jnp.stack([share] + [turn(share, s, 0) for s in (1, 2, 3)])
    pair = after(jnp.where(y == 0, pair, got[0] + got[1] + got[2]), share)
    own = jnp.stack([pair] + [shift(pair, "x", s) for s in (1, 2, 3)])
    cols = [some] + [turn(some, s, 1) for s in (1, 2, 3)]
    corner, inverse = factor_head(place, own, swap(own))
    return update(place, matrix, rows, cols, corner, inverse)


def solution(mesh):
    grid = Mesh(mesh.devices.reshape(4, 4, 8, 2), ("y", "x", "z", "core"))
    spec = P(("y", "x"), ("z", "core"))
    return jax.shard_map(shards, mesh=grid, in_specs=(spec,), out_specs=spec, check_vma=False)
```

```python
import jax
import jax.numpy as jnp
from jax import lax
from jax.experimental import pallas as pl
from jax.experimental.pallas import tpu as pltpu
from jax.sharding import Mesh, PartitionSpec as P

BLOCK = 128
PANELS = 4
SPAN = BLOCK * PANELS
SUB = 8
F32 = jnp.float32
BF16 = jnp.bfloat16


def split(value):
    high = value.astype(BF16)
    low = (value - high.astype(F32)).astype(BF16)
    return high, low


def plain_dot(left, right, left_dim, right_dim):
    return lax.dot_general(
        left, right, (((left_dim,), (right_dim,)), ((), ())), preferred_element_type=F32
    )


def pieces_left(high, low):
    return jnp.concatenate([high, high, low], 1)


def lane_fill(value, lane):
    return jnp.broadcast_to(value[:, lane : lane + 1], (SUB, BLOCK))


def eliminate(a, scratch):
    a = list(a)
    groups = len(a)
    sub = lax.broadcasted_iota(jnp.int32, (SUB, BLOCK), 0)
    lane = lax.broadcasted_iota(jnp.int32, (SUB, BLOCK), 1)
    upper, lower = [None] * groups, [None] * groups
    columns = [lane_fill(a[0], j) for j in range(SUB)]

    def stored_row(at):
        return jnp.broadcast_to(scratch[at : at + 1, :], (SUB, BLOCK))

    for c in range(groups):
        base = SUB * c
        inside = (lane >= base) & (lane < base + SUB)
        at = (c % 2) * (SUB + 1 + SUB) * SUB
        scratch[at : at + SUB, :] = a[c]
        for j in range(SUB):
            scratch[at + SUB * (j + 1) : at + SUB * (j + 2), :] = columns[j]
        s = [
            [stored_row(at + SUB * (j + 1) + i) if i >= j else None for j in range(SUB)]
            for i in range(SUB)
        ]
        rows = [stored_row(at + j) for j in range(SUB)]
        units = [(lane == base + j).astype(F32) for j in range(SUB)]
        more = c + 1 < groups
        if more:
            left = [lane_fill(a[c + 1], base + j) for j in range(SUB)]
            columns = [lane_fill(a[c + 1], base + SUB + j) for j in range(SUB)]
            a[c + 1] = jnp.where(inside, 0.0, a[c + 1])
        inv, merged = [None] * SUB, [None] * SUB
        for j in range(SUB):
            inv[j] = lax.rsqrt(s[j][j])
            for i in range(j + 1, SUB):
                s[i][j] = s[i][j] * inv[j]
            for k in range(j + 1, SUB):
                for i in range(k, SUB):
                    s[i][k] = s[i][k] - s[i][j] * s[k][j]
            rows[j] = rows[j] * inv[j]
            units[j] = units[j] * inv[j]
            for k in range(j + 1, SUB):
                rows[k] = rows[k] - s[k][j] * rows[j]
                units[k] = units[k] - s[k][j] * units[j]
            merged[j] = jnp.where(inside, units[j], rows[j])
            if more:
                left[j] = left[j] * inv[j]
                for k in range(j + 1, SUB):
                    left[k] = left[k] - left[j] * s[k][j]
                a[c + 1] = a[c + 1] - left[j] * merged[j]
                spot = at + (SUB + 1 + j) * SUB
                scratch[spot : spot + SUB, :] = left[j]
                for k in range(SUB):
                    columns[k] = columns[k] - left[j] * stored_row(spot + k)
        upper[c], lower[c] = rows[0], merged[0]
        for j in range(1, SUB):
            upper[c] = jnp.where(sub == j, rows[j], upper[c])
            lower[c] = jnp.where(sub == j, merged[j], lower[c])
        if c + 2 < groups:
            solved = list(merged)
            for j in range(SUB - 1, -1, -1):
                solved[j] = solved[j] * inv[j]
                for k in range(j):
                    solved[k] = solved[k] - s[j][k] * solved[j]
            for g in range(c + 2, groups):
                value = jnp.where(inside, 0.0, a[g])
                for j in range(SUB):
                    value = value - lane_fill(a[g], base + j) * solved[j]
                a[g] = value
    return upper, lower


def split3(value):
    high = value.astype(BF16)
    rest = value - high.astype(F32)
    middle = rest.astype(BF16)
    low = (rest - middle.astype(F32)).astype(BF16)
    return high, middle, low


def stack_left(value):
    high, middle, low = split3(value)
    return jnp.concatenate([high, high, middle, middle, high, low], 1)


def stack_right(value):
    high, middle, low = split3(value)
    return jnp.concatenate([high, middle, high, middle, low, high], 0)


def stacked_dot(left, right):
    return lax.dot_general(left, right, (((1,), (0,)), ((), ())), preferred_element_type=F32)


def head_kernel(place, own, other, corner, v_ref, head, u_ref, scratch):
    x, c = place[1], place[3]
    half = SPAN // 2
    for step in range(PANELS):
        rows = pl.ds(pl.multiple_of(((x - step + PANELS) % PANELS) * BLOCK, BLOCK), BLOCK)
        for n in range(2):
            block = slice(n * BLOCK, (n + 1) * BLOCK)
            at = pl.multiple_of(c * half + n * BLOCK, BLOCK)
            head[rows, pl.ds(at, BLOCK)] = own[step, block]
            at = pl.multiple_of((1 - c) * half + n * BLOCK, BLOCK)
            head[rows, pl.ds(at, BLOCK)] = other[step, block]
    row = lax.broadcasted_iota(jnp.int32, (BLOCK, BLOCK), 0)
    col = lax.broadcasted_iota(jnp.int32, (BLOCK, BLOCK), 1)
    spans = [slice(k * BLOCK, (k + 1) * BLOCK) for k in range(PANELS)]
    work = {(i, j): head[spans[i], spans[j]] for i in range(PANELS) for j in range(i, PANELS)}
    unit = {}
    for k in range(PANELS):
        block = work[k, k]
        upper, lower = eliminate([block[g : g + SUB] for g in range(0, BLOCK, SUB)], scratch)
        factor = jnp.where(row <= col, jnp.concatenate(upper, 0), 0.0)
        inverse = jnp.where(row >= col, jnp.concatenate(lower, 0), 0.0)
        u_ref[spans[k], spans[k]] = factor
        v_ref[spans[k], spans[k]] = inverse
        sources = [work[k, j] for j in range(k + 1, PANELS)] + [unit[k, j] for j in range(k)]
        solved = stacked_dot(stack_left(inverse), stack_right(jnp.concatenate(sources, 1)))
        pieces = [solved[:, spans[i]] for i in range(PANELS - 1)]
        right = {j: pieces[j - k - 1] for j in range(k + 1, PANELS)}
        left = {j: pieces[PANELS - 1 - k + j] for j in range(k)}
        for j, value in right.items():
            u_ref[spans[k], spans[j]] = value
        for j, value in left.items():
            v_ref[spans[k], spans[j]] = value
        left[k] = inverse
        for i in range(k + 1, PANELS):
            factors = stack_left(right[i].T)
            first = i
            if i == k + 1:
                work[i, i] = work[i, i] - stacked_dot(factors, stack_right(right[i]))
                first = i + 1
            values = [right[j] for j in range(first, PANELS)] + [left[j] for j in range(k + 1)]
            change = stacked_dot(factors, stack_right(jnp.concatenate(values, 1)))
            parts = [change[:, n * BLOCK : (n + 1) * BLOCK] for n in range(len(values))]
            for j in range(first, PANELS):
                work[i, j] = work[i, j] - parts.pop(0)
            for j in range(k + 1):
                part = parts.pop(0)
                unit[i, j] = unit[i, j] - part if (i, j) in unit else -part
    for i in range(PANELS):
        for j in range(i):
            u_ref[spans[i], spans[j]] = jnp.zeros((BLOCK, BLOCK), F32)
            v_ref[spans[j], spans[i]] = jnp.zeros((BLOCK, BLOCK), F32)
    q = jnp.minimum(2 * place[2] + c, PANELS - 1)
    at_row = pl.ds(pl.multiple_of(q * BLOCK, BLOCK), BLOCK)
    corner[...] = u_ref[at_row, pl.ds(pl.multiple_of(x * BLOCK, BLOCK), BLOCK)].T


def factor_head(place, own, other):
    shapes = [jax.ShapeDtypeStruct((n, n), F32) for n in (BLOCK, SPAN)]
    vmem = pl.BlockSpec(memory_space=pltpu.VMEM)
    return pl.pallas_call(
        head_kernel,
        out_shape=shapes,
        in_specs=[pl.BlockSpec(memory_space=pltpu.SMEM), vmem, vmem],
        out_specs=[vmem, vmem],
        scratch_shapes=[
            pltpu.VMEM((SPAN, SPAN), F32),
            pltpu.VMEM((SPAN, SPAN), F32),
            pltpu.VMEM((2 * (2 * SUB + 1) * SUB, BLOCK), F32),
        ],
        cost_estimate=pl.CostEstimate(
            flops=30_000_000_000, transcendentals=0, bytes_accessed=4 * 2**20
        ),
        compiler_params=pltpu.CompilerParams(vmem_limit_bytes=48 * 2**20),
    )(place, own, other)


SLAB = BLOCK // 4


def after(value, ready):
    return value + ready[(slice(0, 1),) * ready.ndim].reshape((1,) * value.ndim) * 0.0


TILE = 256


def update_kernel(
    place, a_ref, rows0, rows1, rows2, rows3, c0, c1, c2, c3, corner, v_ref, out_ref, column, w_all, v_all
):
    y, x, z, c = place[0], place[1], place[2], place[3]
    t = pl.program_id(0)
    half = SPAN // 2

    @pl.when(t == 0)
    def _():
        for late, ref in enumerate((c0, c1, c2, c3)):
            for early in range(4):
                dx = jnp.where(c == 0, early, late)
                dy = jnp.where(c == 0, late, early)
                at = ((x - dx + 4) % 4) * BLOCK + ((y - dy + 4) % 4) * SLAB
                column[pl.ds(pl.multiple_of(at, SLAB), SLAB), :] = ref[early]
        v_high, v_low = split(v_ref[...])
        high, low = split(column[...])
        for i in range(2):
            rows, depth = slice(i * half, (i + 1) * half), (i + 1) * half
            left = pieces_left(v_high[rows, :depth], v_low[rows, :depth])
            right = jnp.concatenate([high[:depth], low[:depth], high[:depth]], 0)
            w_high, w_low = split(plain_dot(left, right, 1, 0))
            for n, value in enumerate((w_high, w_low, w_high)):
                w_all[n * SPAN + i * half : n * SPAN + (i + 1) * half] = value
            v_all[i, :, : 3 * depth] = jnp.concatenate(
                [v_high[rows, :depth], v_low[rows, :depth], v_high[rows, :depth]], 1
            )

    rows = jnp.concatenate([rows0[0], rows1[0], rows2[0], rows3[0]], 1)
    high, low = split(rows)
    panel = jnp.concatenate(
        [
            plain_dot(pieces_left(high[:, :half], low[:, :half]), v_all[0, :, : 3 * half], 1, 1),
            plain_dot(pieces_left(high, low), v_all[1], 1, 1),
        ],
        1,
    )
    high, low = split(panel)
    out_ref[...] = a_ref[...] - plain_dot(pieces_left(high, low), w_all[...], 1, 0)
    q = 2 * z + c
    for k in range(PANELS):

        @pl.when(q == k)
        def _():
            out_ref[:, :BLOCK] = panel[:, k * BLOCK : (k + 1) * BLOCK]

    @pl.when((t == 0) & (y == 0))
    def _():
        out_ref[:BLOCK, :] = jnp.zeros((BLOCK, out_ref.shape[1]), F32)

    @pl.when((t == 0) & (y == 0) & (q < PANELS))
    def _():
        out_ref[:BLOCK, :BLOCK] = corner[...]


def update(place, matrix, rows, cols, corner, inverse):
    height, width = matrix.shape
    vmem = pl.BlockSpec(memory_space=pltpu.VMEM)
    tile = pl.BlockSpec((TILE, width), lambda t, place: (t, 0))
    part = (1,) + rows.shape[1:]

    def whole(shape):
        return pl.BlockSpec(shape, lambda t, place: (0,) * len(shape), pipeline_mode=pl.Buffered(1))

    pieces = [
        pl.BlockSpec(part, lambda t, place: (2 * t, 0, 0)),
        pl.BlockSpec(part, lambda t, place: (jnp.where(t == 0, 8, 16 - 2 * t), 0, 0)),
        pl.BlockSpec(part, lambda t, place: (jnp.where(t == 0, 11, 3 + 2 * t), 0, 0)),
        pl.BlockSpec(part, lambda t, place: (2 * ((9 - t) % 8) + 1, 0, 0)),
    ]
    return pl.pallas_call(
        update_kernel,
        out_shape=jax.ShapeDtypeStruct(matrix.shape, F32),
        grid_spec=pltpu.PrefetchScalarGridSpec(
            num_scalar_prefetch=1,
            grid=(height // TILE,),
            in_specs=[tile] + pieces + [vmem] * 4 + [vmem, vmem],
            out_specs=tile,
            scratch_shapes=[
                pltpu.VMEM((SPAN, width), F32),
                pltpu.VMEM((3 * SPAN, width), BF16),
                pltpu.VMEM((2, SPAN // 2, 3 * SPAN), BF16),
            ],
        ),
        compiler_params=pltpu.CompilerParams(vmem_limit_bytes=52 * 2**20),
    )(place, matrix, rows, rows, rows, rows, *cols, corner, inverse)


def send(value, axis, pairs):
    return lax.ppermute(value, axis, pairs)


def shift(value, axis, step):
    size = lax.axis_size(axis)
    return lax.ppermute(value, axis, [(i, (i + step) % size) for i in range(size)])


def swap(value):
    return lax.ppermute(value, "core", [(0, 1), (1, 0)])


def turn(value, step, first):
    pairs = []
    for y in range(4):
        for x in range(4):
            for core in range(2):
                to = (y, (x + step) % 4) if core == first else ((y + step) % 4, x)
                pairs.append(((y * 4 + x) * 2 + core, (to[0] * 4 + to[1]) * 2 + core))
    return lax.ppermute(value, ("y", "x", "core"), pairs)


def shards(matrix):
    y, x = lax.axis_index("y"), lax.axis_index("x")
    z, c = lax.axis_index("z"), lax.axis_index("core")
    place = jnp.stack([y, x, z, c]).astype(jnp.int32)

    head = matrix[:BLOCK, :BLOCK]
    twin = swap(head)
    pair = jnp.concatenate([jnp.where(c == 0, head, twin), jnp.where(c == 0, twin, head)], 0)
    pairs = [[] for _ in range(4)]
    for (source_z, source_c), targets in (
        ((0, 0), (1, 2, 3)),
        ((0, 1), (7, 6, 5, 4)),
        ((1, 0), (2, 3, 4, 5)),
        ((1, 1), (0, 7, 6)),
    ):
        for n, target in enumerate(targets):
            pairs[n].append((source_z * 2 + source_c, target * 2 + source_z))
    quarter = matrix.shape[0] // 4
    lead = [matrix[n * quarter : (n + 1) * quarter, :BLOCK] for n in range(4)]
    got = [
        lax.ppermute(jnp.concatenate([pair, lead[(n + 1) % 4]], 0), ("z", "core"), group)
        for n, group in enumerate(pairs)
    ]
    mine = jnp.where(z == c, jnp.concatenate([pair, lead[0]], 0), got[0] + got[1] + got[2] + got[3])
    pair, part = mine[: 2 * BLOCK], mine[2 * BLOCK :]
    rows = lax.all_gather(part, ("z", "core"))

    top = matrix[:BLOCK]
    sent = [send(top[m * SLAB : (m + 1) * SLAB], "y", [(0, m)]) for m in (1, 2, 3)]
    share = jnp.where(y == 0, top[:SLAB], sent[0] + sent[1] + sent[2])

    got = [send(pair, "y", [(0, m)]) for m in (1, 2, 3)]
    some = jnp.stack([share] + [turn(share, s, 0) for s in (1, 2, 3)])
    pair = after(jnp.where(y == 0, pair, got[0] + got[1] + got[2]), share)
    own = jnp.stack([pair] + [shift(pair, "x", s) for s in (1, 2, 3)])
    cols = [some] + [turn(some, s, 1) for s in (1, 2, 3)]
    corner, inverse = factor_head(place, own, swap(own))
    return update(place, matrix, rows, cols, corner, inverse)


def solution(mesh):
    grid = Mesh(mesh.devices.reshape(4, 4, 8, 2), ("y", "x", "z", "core"))
    spec = P(("y", "x"), ("z", "core"))
    return jax.shard_map(shards, mesh=grid, in_specs=(spec,), out_specs=spec, check_vma=False)
```
